512 devices in a mesh: pb: 32 (over x_lo, z), ka: 16 (over y, x_hi, core).
Axes of the slice: x: 4 (x_hi: 2, x_lo: 2; x = x_hi * 2 + x_lo), y: 4, z: 16, core: 2. Of those that a mesh axis runs over, the one named last changes fastest.
Arguments:
- segments: float32 [8192, 1024], P(('pb', 'ka')), may hold values from -0.25 to 0.25
- futures: float32 [8192, 1024], P(('pb', 'ka')), may hold values from -0.25 to 0.25
- pair_index: int32 [8192], P('pb'), may hold values from 0 to 8191, each once
- log_scale: float32 [1], replicated, may hold values from 1.5 to 2.5
- logit_bias: float32 [1], replicated, may hold values from -7 to -5
Outputs:
- grad_segments: float32 [8192, 1024], P(('pb', 'ka'))
- grad_futures: float32 [8192, 1024], P(('pb', 'ka'))
- scalar_values: float32 [3], replicated
The draws below stay inside these ranges and needn't reach their ends.
Inputs may be any that keep to these rules, and one draw needn't show every extreme that they name: `pair_index`: every key row is the positive of exactly one query row.
All inputs are finite; a program needn't handle non-finite values.
Results may differ from the reference program's by a relative error of at most 0.0003.
Values sent between devices are 32-bit elements; how exact they have to be, the bound alone decides.
A program may use at most 64 MiB of HBM per device.

```python
import jax
import jax.numpy as jnp
from jax import lax

D = 1024
ROWS = 8192


def shard_levels(key, extent, shards, least, largest):
    def one(axis_at, parts):
        heights = jax.random.uniform(jax.random.fold_in(jax.random.fold_in(key, 6), axis_at), (parts,), jnp.float32, least / len(shards), largest / len(shards))
        return jnp.repeat(jnp.exp(heights), extent[axis_at] // parts).reshape((-1,) + (1,) * (len(extent) - axis_at - 1))

    loudness = one(*shards[0])
    for cut in shards[1:]:
        loudness = loudness * one(*cut)
    return loudness


def noise(own_key, dims, scale, limit, cuts=(), kind=jnp.bfloat16):
    drawn = jax.random.normal(own_key, dims, jnp.float32) * scale
    if len(cuts) > 0:
        drawn = shard_levels(own_key, dims, cuts, -0.22, 0.18) * drawn
    return jnp.clip(drawn, min=-limit, max=limit).astype(kind)


def setup_inputs(seed: int = 0) -> dict:
    keys = jax.random.split(jax.random.key(seed), 6)
    return {
        "segments": noise(keys[0], (ROWS, D), 0.03125, 0.25, ((0, 512),), jnp.float32),
        "futures": noise(keys[1], (ROWS, D), 0.03125, 0.25, ((0, 512),), jnp.float32),
        "pair_index": jax.random.permutation(keys[2], ROWS).astype(jnp.int32),
        "log_scale": jnp.clip(jax.random.uniform(keys[3], (1,), jnp.float32, 1.5, 2.5), 1.5, 2.5),
        "logit_bias": jnp.clip(jax.random.uniform(keys[4], (1,), jnp.float32, -7.0, -5.0), -7.0, -5.0),
    }


epsilon = 1e-06

def unit_rows(matrix):
    inverse = lax.rsqrt(lax.optimization_barrier(jnp.sum(matrix * matrix, axis=1, keepdims=True)) + epsilon)
    return (matrix * inverse, inverse)

def backward_norm(direction, grad_dir, inverse):
    return (grad_dir - direction * lax.optimization_barrier(jnp.sum(direction * grad_dir, axis=1, keepdims=True))) * inverse

def reference(segments, futures, pair_index, log_scale, logit_bias):
    query_unit, query_inv = unit_rows(segments)
    key_unit, key_inv = unit_rows(futures)
    scale_value = jnp.exp(log_scale[0])
    offset_value = logit_bias[0]
    block_rows = min(512, ROWS)
    block_count = ROWS // block_rows
    key_columns = jnp.arange(ROWS, dtype=jnp.int32)

    def advance(carry, block_id):
        key_acc, total_acc = carry
        first_row = (block_id * block_rows).astype(jnp.int32)
        query_part = lax.dynamic_slice_in_dim(query_unit, first_row, block_rows, 0)
        pair_part = lax.dynamic_slice_in_dim(pair_index, first_row, block_rows, 0)
        logits = scale_value * jnp.dot(query_part, key_unit.T, precision=lax.Precision.HIGHEST) + offset_value
        hitmask = key_columns[None, :] == pair_part[:, None]
        weights = jax.nn.sigmoid(logits) - hitmask.astype(jnp.float32)
        partial_value = jnp.stack([jnp.sum(jax.nn.softplus(logits)) - jnp.sum(jnp.where(hitmask, logits, jnp.float32(0.0))), jnp.sum(weights * (logits - offset_value)), jnp.sum(weights)])
        query_terms = scale_value * jnp.dot(weights, key_unit, precision=lax.Precision.HIGHEST)
        key_acc = key_acc + scale_value * jnp.dot(weights.T, query_part, precision=lax.Precision.HIGHEST)
        return ((key_acc, total_acc + partial_value), query_terms)
    initial = (jnp.zeros((ROWS, D), jnp.float32), jnp.zeros((3,), jnp.float32))
    (key_grad, totals), query_blocks = lax.scan(advance, initial, jnp.arange(block_count, dtype=jnp.int32))
    query_grad = query_blocks.reshape(ROWS, D)
    grad_segments = backward_norm(query_unit, query_grad, query_inv)
    grad_futures = backward_norm(key_unit, key_grad, key_inv)
    return (grad_segments, grad_futures, totals / ROWS)
```

```python
import jax
import jax.numpy as jnp
from jax import lax
from jax.experimental import pallas as pl
from jax.experimental.pallas import tpu as pltpu
from jax.sharding import PartitionSpec as P

MESH = pl.DeviceIdType.MESH
f32 = jnp.float32
bf16 = jnp.bfloat16
epsilon = 1e-06

NX, NY, NZ = 4, 4, 16
CHIPS = NX * NY
ROWS = 16
WIDTH = 1024
QUERIES = CHIPS * 2 * ROWS
KEYS = NZ * ROWS
FIRST = 12
HALVES = 2
HALF = ROWS // HALVES


def coordinates():
    pb = lax.axis_index("pb")
    ka = lax.axis_index("ka")
    return lax.rem(ka // 2, 2) * 2 + pb // NZ, ka // 4, lax.rem(pb, NZ), lax.rem(ka, 2)


def device(x, y, z, core):
    return (lax.rem(x, 2) * NZ + z, y * 4 + (x // 2) * 2 + core)


def chip_index(x, y):
    return lax.rem(x, 2) * 8 + y * 2 + x // 2


def chip_place(index):
    return (index % 2) * 2 + index // 8, (index // 2) % 4


def place_up(step):
    return 0 if step == 0 else 2 * step - 1


def place_down(step):
    return 2 * step


def split(value):
    high = value.astype(bf16)
    return high, (value - high.astype(f32)).astype(bf16)


def dot(a, b, dims):
    return lax.dot_general(a, b, (dims, ((), ())), preferred_element_type=f32)


def dot3(a_high, a_low, b_high, b_low, dims):
    return (dot(a_low, b_high, dims) + dot(a_high, b_low, dims)) + dot(a_high, b_high, dims)


NN = ((1,), (0,))
NT = ((1,), (1,))


def fold(value):
    rows = jnp.sum(value, axis=0, keepdims=True)
    return rows[:, 0:128] + rows[:, 128:256] + rows[:, 256:384] + rows[:, 384:512]


def unit_rows(value):
    inverse = lax.rsqrt(jnp.sum(value * value, axis=1, keepdims=True) + epsilon)
    return value * inverse, inverse


def kernel(
    segments, futures, pairs, log_scale, logit_bias,
    grad_segments, grad_futures, scalars,
    queries, queries_high, queries_low, keys, keys_high, keys_low,
    logits, weights, key_terms, query_terms,
    sums_up, sums_down, sibling_terms, plane_terms, targets,
    sums_mine, sums_pair, sums_plane, sums_line,
    gz_send, gz_recv, gp_send, gp_recv, gf_send, gf_recv, t_sem,
    rz_send, rz_recv, rs_send, rs_recv, rp_send, rp_recv,
    sp_sem, sl_send, sl_recv, sz_send, sz_recv,
):
    x, y, z, core = coordinates()
    me = chip_index(x, y)
    up = device(x, y, lax.rem(z + 1, NZ), core)
    down = device(x, y, lax.rem(z + NZ - 1, NZ), core)
    sibling = device(x, y, z, 1 - core)

    def remote(src, dst, send, recv, to):
        return pltpu.make_async_remote_copy(
            src_ref=src, dst_ref=dst, send_sem=send, recv_sem=recv, device_id=to, device_id_type=MESH
        )

    def plane_device(offset, other=False):
        return device(
            lax.rem(x + offset // 4, NX), lax.rem(y + offset % 4, NY), z, 1 - core if other else core
        )

    def plane_source(offset):
        return chip_index(lax.rem(x - offset // 4 + NX, NX), lax.rem(y - offset % 4 + NY, NY))

    sent = []

    def start(copy):
        copy.start()
        sent.append(copy)

    query_unit, query_inverse = unit_rows(segments[...])
    key_unit, key_inverse = unit_rows(futures[...])
    queries[me * 2 + core] = query_unit
    keys[0] = key_unit
    targets[lax.rem(x, 2)] = pairs[...]

    barrier = pltpu.get_barrier_semaphore()
    offsets = [1, 3, 4, 12, 5, 7, 13, 15, 2, 8, 6, 14, 9, 11, 10]
    greeted = [up, down, sibling] + [plane_device(d) for d in offsets]
    for other in greeted:
        pl.semaphore_signal(barrier, inc=1, device_id=other, device_id_type=MESH)
    pl.semaphore_wait(barrier, len(greeted))

    def gather_z(way, step, half):
        source = (place_up if way == 0 else place_down)(step - 1)
        target = (place_up if way == 0 else place_down)(step)
        rows = pl.ds(half * HALF, HALF)
        return remote(
            keys.at[source, rows], keys.at[target, rows],
            gz_send.at[way, step - 1, half], gz_recv.at[way, step - 1, half], up if way == 0 else down,
        )

    def gather_plane(offset):
        slot = queries.at[me * 2 + core]
        return remote(slot, slot, gp_send.at[offset], gp_recv.at[offset], plane_device(offset))

    def forward(offset):
        slot = queries.at[plane_source(offset) * 2 + core]
        return remote(slot, slot, gf_send.at[offset], gf_recv.at[offset], sibling)

    def step_z(step):
        for half in range(HALVES):
            for way in range(2):
                if way == 1 and step > 7:
                    continue
                if step > 1:
                    gather_z(way, step - 1, half).wait_recv()
                start(gather_z(way, step, half))

    step_z(1)
    start(forward(0))
    mine = targets.at[lax.rem(x, 2)]
    target_copy = remote(
        mine, mine, t_sem.at[0], t_sem.at[1], device(x + 1 - 2 * lax.rem(x, 2), y, z, core)
    )
    start(target_copy)
    for d in offsets:
        start(gather_plane(d))

    scale = jnp.exp(log_scale[...])
    bias = logit_bias[...]

    arrivals = list(offsets)

    def forward_next(count):
        for _ in range(min(count, len(arrivals))):
            d = arrivals.pop(0)
            gather_plane(d).wait_recv()
            start(forward(d))

    for step in range(2, 9):
        step_z(step)
        if step >= 4:
            forward_next(4)
    forward_next(15)
    target_copy.wait_recv()
    for d in [0] + offsets:
        forward(d).wait_recv()

    def split_keys(first, last):
        high, low = split(keys[first:last].reshape((last - first) * ROWS, WIDTH))
        keys_high[first * ROWS : last * ROWS] = high
        keys_low[first * ROWS : last * ROWS] = low

    def split_queries(first, last):
        high, low = split(queries[first:last].reshape((last - first) * ROWS, WIDTH))
        queries_high[first * ROWS : last * ROWS] = high
        queries_low[first * ROWS : last * ROWS] = low

    for i in range(0, 32, 8):
        split_queries(i, i + 8)
    split_keys(0, FIRST)

    def pair_block(first, last):
        a, b = first * ROWS, last * ROWS
        raw = dot3(
            keys_high[a:b], keys_low[a:b], queries_high[...], queries_low[...], NT
        )
        value = scale * raw + bias
        row = lax.broadcasted_iota(jnp.int32, (b - a, 1), 0) + a
        place = row // ROWS
        step = (place + 1) // 2
        line = lax.rem(z + jnp.where(place % 2 == 1, NZ - step, step), NZ)
        ka = lax.axis_index("ka")
        key_row = (lax.rem(x, 2) * NZ + line) * (ROWS * 16) + ka * ROWS + row % ROWS
        target = jnp.concatenate([targets[0], targets[1]], axis=1)
        hit = key_row == target
        small = jnp.exp(-jnp.abs(value))
        sigmoid = jnp.where(value >= 0, f32(1.0), small) / (f32(1.0) + small)
        weight = sigmoid - hit.astype(f32)
        softplus = jnp.maximum(value, f32(0.0)) + jnp.log1p(small)
        weights[a:b] = scale * weight
        loss = fold(softplus - jnp.where(hit, value, f32(0.0)))
        by_scale = fold(weight * (value - bias))
        by_bias = fold(weight)
        return jnp.concatenate([loss, by_scale, by_bias, jnp.zeros((5, 128), f32)], axis=0)

    def key_block(first, last):
        a, b = first * ROWS, last * ROWS
        high, low = split(weights[a:b])
        out = dot3(high, low, queries_high[...], queries_low[...], NN)
        key_terms[first:last] = out.reshape(last - first, ROWS, WIDTH)

    totals = pair_block(0, FIRST)
    for half in range(HALVES):
        gather_z(0, 8, half).wait_recv()
        gather_z(1, 7, half).wait_recv()
    split_keys(FIRST, NZ)
    totals = totals + pair_block(FIRST, NZ)
    key_block(FIRST, NZ)

    def sum_z(way, step, half):
        rows = pl.ds(half * HALF, HALF)
        if way == 0:
            place = place_down(8 - step) if step > 0 else place_up(8)
            land = sums_up
        else:
            place = place_up(7 - step)
            land = sums_down
        return place, land, remote(
            key_terms.at[place, rows], land.at[step, rows],
            rz_send.at[way, step, half], rz_recv.at[way, step, half], up if way == 0 else down,
        )

    def reduce_z(step):
        for half in range(HALVES):
            rows = slice(half * HALF, half * HALF + HALF)
            for way in range(2):
                if way == 1 and step > 6:
                    continue
                place, land, copy = sum_z(way, step, half)
                if step > 0:
                    sum_z(way, step - 1, half)[2].wait_recv()
                    key_terms[place, rows] = key_terms[place, rows] + land[step - 1, rows]
                start(copy)

    reduce_z(0)

    sums_mine[...] = totals
    pair_sums = remote(sums_mine, sums_pair, sp_sem.at[0], sp_sem.at[1], sibling)
    start(pair_sums)

    key_block(0, FIRST)
    reduce_z(1)

    def query_block(first, last):
        a, b = first * 2 * ROWS, last * 2 * ROWS
        high, low = split(weights[:, a:b].T)
        out = dot3(high, low, keys_high[...], keys_low[...], NN)
        query_terms[first:last] = out.reshape(last - first, 2, ROWS, WIDTH)

    def sum_sibling(index):
        return remote(
            query_terms.at[index, 1 - core], sibling_terms.at[index], rs_send.at[index], rs_recv.at[index], sibling
        )

    def sum_plane(index):
        cx, cy = chip_place(index)
        return remote(
            query_terms.at[index, core], plane_terms.at[me], rp_send.at[index], rp_recv.at[me],
            device(jnp.int32(cx), jnp.int32(cy), z, core),
        )

    def plane_arrival(index):
        return remote(
            query_terms.at[index, core], plane_terms.at[index], rp_send.at[index], rp_recv.at[index], sibling
        )

    def send_plane(first, last):
        for index in range(first, last):
            sum_sibling(index).wait_recv()
            query_terms[index, core] = query_terms[index, core] + sibling_terms[index]

            @pl.when(index != me)
            def _():
                sum_plane(index).start()

    GROUP = 4
    for first in range(0, CHIPS, GROUP):
        query_block(first, first + GROUP)
        for index in range(first, first + GROUP):
            start(sum_sibling(index))
        if first >= GROUP:
            send_plane(first - GROUP, first)
        if first % (2 * GROUP) == GROUP:
            reduce_z(2 + first // (2 * GROUP))
        if first == 0:
            pair_sums.wait_recv()
            sums_plane[me] = sums_mine[...] + sums_pair[...]
            for d in offsets:
                start(remote(sums_plane.at[me], sums_plane.at[me], sl_send.at[d], sl_recv.at[d], plane_device(d)))
    send_plane(CHIPS - GROUP, CHIPS)
    reduce_z(4)
    for d in offsets:
        slot = sums_plane.at[plane_source(d)]
        remote(slot, slot, sl_send.at[d], sl_recv.at[d], sibling).wait_recv()
    sums_line[z] = jnp.sum(sums_plane[...], axis=0)
    for d in range(1, NZ):
        slot = sums_line.at[z]
        start(remote(slot, slot, sz_send.at[d], sz_recv.at[d], device(x, y, lax.rem(z + d, NZ), core)))
    reduce_z(5)
    reduce_z(6)
    reduce_z(7)

    def backward(direction, grad, inverse):
        return (grad - direction * jnp.sum(direction * grad, axis=1, keepdims=True)) * inverse

    plane_terms[me] = query_terms[me, core]
    for index in range(CHIPS):

        @pl.when(index != me)
        def _():
            plane_arrival(index).wait_recv()

    query_grad = jnp.sum(plane_terms[...], axis=0)
    grad_segments[...] = backward(query_unit, query_grad, query_inverse)

    for d in range(1, NZ):
        slot = sums_line.at[lax.rem(z - d + NZ, NZ)]
        remote(slot, slot, sz_send.at[d], sz_recv.at[d], sibling).wait_recv()
    total = jnp.sum(sums_line[...], axis=0) * f32(1.0 / 8192)
    for i in range(3):
        scalars[i] = jnp.sum(total[i : i + 1, :])

    for half in range(HALVES):
        sum_z(0, 7, half)[2].wait_recv()
        sum_z(1, 6, half)[2].wait_recv()
    key_grad = key_terms[0] + sums_up[7] + sums_down[6]
    grad_futures[...] = backward(key_unit, key_grad, key_inverse)

    for copy in sent:
        copy.wait_send()
    for index in range(CHIPS):

        @pl.when(index != me)
        def _():
            sum_plane(index).wait_send()


def per_device(segments, futures, pair_index, log_scale, logit_bias):
    dma = pltpu.SemaphoreType.DMA
    vmem = pltpu.VMEM
    block = (ROWS, WIDTH)
    in_vmem = pl.BlockSpec(memory_space=pltpu.VMEM)
    return pl.pallas_call(
        kernel,
        out_shape=(
            jax.ShapeDtypeStruct(block, f32),
            jax.ShapeDtypeStruct(block, f32),
            jax.ShapeDtypeStruct((3,), f32),
        ),
        in_specs=[in_vmem] * 5,
        out_specs=(in_vmem, in_vmem, pl.BlockSpec(memory_space=pltpu.SMEM)),
        scratch_shapes=[
            vmem((CHIPS * 2,) + block, f32),
            vmem((QUERIES, WIDTH), bf16),
            vmem((QUERIES, WIDTH), bf16),
            vmem((NZ,) + block, f32),
            vmem((KEYS, WIDTH), bf16),
            vmem((KEYS, WIDTH), bf16),
            vmem((KEYS, QUERIES), f32),
            vmem((KEYS, QUERIES), f32),
            vmem((NZ,) + block, f32),
            vmem((CHIPS, 2) + block, f32),
            vmem((8,) + block, f32),
            vmem((8,) + block, f32),
            vmem((CHIPS,) + block, f32),
            vmem((CHIPS,) + block, f32),
            vmem((2, 1, 256), jnp.int32),
            vmem((8, 128), f32),
            vmem((8, 128), f32),
            vmem((CHIPS, 8, 128), f32),
            vmem((NZ, 8, 128), f32),
            dma((2, 8, HALVES)), dma((2, 8, HALVES)),
            dma((CHIPS,)), dma((CHIPS,)),
            dma((CHIPS,)), dma((CHIPS,)),
            dma((2,)),
            dma((2, 8, HALVES)), dma((2, 8, HALVES)),
            dma((CHIPS,)), dma((CHIPS,)),
            dma((CHIPS,)), dma((CHIPS,)),
            dma((2,)),
            dma((CHIPS,)), dma((CHIPS,)),
            dma((NZ,)), dma((NZ,)),
        ],
        compiler_params=pltpu.CompilerParams(
            collective_id=0, has_side_effects=True, vmem_limit_bytes=40 << 20
        ),
    )(
        segments,
        futures,
        pair_index.reshape(1, 256),
        log_scale.reshape(1, 1),
        logit_bias.reshape(1, 1),
    )


def solution(mesh):
    in_specs = (P(("pb", "ka"), None), P(("pb", "ka"), None), P("pb"), P(), P())
    out_specs = (P(("pb", "ka"), None), P(("pb", "ka"), None), P())
    return jax.shard_map(
        per_device, mesh=mesh, in_specs=in_specs, out_specs=out_specs, check_vma=False
    )
```

```python
import jax
import jax.numpy as jnp
from jax import lax
from jax.experimental import pallas as pl
from jax.experimental.pallas import tpu as pltpu
from jax.sharding import PartitionSpec as P

MESH = pl.DeviceIdType.MESH
f32 = jnp.float32
bf16 = jnp.bfloat16
epsilon = 1e-06

NX, NY, NZ = 4, 4, 16
RING = NZ // 2
ROWS = 16
WIDTH = 1024
CHIPS = 16
QUERIES = CHIPS * 2 * ROWS
KEYS = CHIPS * ROWS
FIRST = 10
HALVES = 2
HALF = ROWS // HALVES
FAR = 4
KZ, KX, QP, QY, QS, TG, RX, RZ, RS, RY, RP, SL, SW, SR, SY = range(15)


def coordinates():
    pb = lax.axis_index("pb")
    ka = lax.axis_index("ka")
    return lax.rem(ka // 2, 2) * 2 + pb // NZ, ka // 4, lax.rem(pb, NZ), lax.rem(ka, 2)


def device(x, y, z, core):
    return (lax.rem(x, 2) * NZ + z, y * 4 + (x // 2) * 2 + core)


def place_of(way, step):
    return 0 if step == 0 else 7 if step == FAR else 2 * step - 1 + way


def has(way, step, half):
    return step < FAR or way == half


def split(value):
    high = value.astype(bf16)
    return high, (value - high.astype(f32)).astype(bf16)


def dot(a, b, dims):
    return lax.dot_general(a, b, (dims, ((), ())), preferred_element_type=f32)


def dot3(a_high, a_low, b_high, b_low, dims):
    return (dot(a_low, b_high, dims) + dot(a_high, b_low, dims)) + dot(a_high, b_high, dims)


NN = ((1,), (0,))
NT = ((1,), (1,))


def fold(value):
    rows = jnp.sum(value, axis=0, keepdims=True)
    return rows[:, 0:128] + rows[:, 128:256] + rows[:, 256:384] + rows[:, 384:512]


def unit_rows(value):
    inverse = lax.rsqrt(jnp.sum(value * value, axis=1, keepdims=True) + epsilon)
    return value * inverse, inverse


def backward(direction, grad, inverse):
    return (grad - direction * jnp.sum(direction * grad, axis=1, keepdims=True)) * inverse


def kernel(
    segments_hbm, futures_hbm, pairs_hbm, log_scale, logit_bias,
    grad_segments, grad_futures, scalars,
    segments, futures, pairs,
    queries, queries_high, queries_low, keys, keys_high, keys_low,
    weights, weights_high, weights_low, key_terms, x_terms, ring_terms,
    query_terms, sibling_terms, y_terms, pair_terms, z_terms, targets,
    sums_line, sums_two, sums_row, sums_y,
    in_sem, send, kz_recv, kx_recv, qp_recv, qy_recv, qs_recv,
    rx_recv, rz_recv, rs_recv, ry_recv, rp_recv, once_recv,
):
    x, y, z, core = coordinates()
    odd_x, odd_z = lax.rem(x, 2), lax.rem(z, 2)
    key_x = x + 1 - 2 * odd_x
    query_x = lax.rem(x + 2 * odd_x + NX - 1, NX)
    pair_z = z + 1 - 2 * odd_z

    sibling = device(x, y, z, 1 - core)
    key_partner = device(key_x, y, z, core)
    query_partner = device(query_x, y, z, core)
    z_partner = device(x, y, pair_z, core)

    def y_device(offset):
        return device(x, lax.rem(y + offset, NY), z, core)

    def ring_device(steps, column=None):
        return device(x if column is None else column, y, lax.rem(z + 2 * steps + NZ, NZ), core)

    def row_device(offset, other):
        return device(lax.rem(x + offset, NX), y, z, 1 - core if other else core)

    def remote(src, dst, kind, recv, to):
        return pltpu.make_async_remote_copy(
            src_ref=src, dst_ref=dst, send_sem=send.at[kind], recv_sem=recv, device_id=to, device_id_type=MESH
        )

    def await_recv(ref, kind, recv):
        remote(ref, ref, kind, recv, sibling).wait_recv()

    def await_send(ref, kind):
        remote(ref, ref, kind, once_recv.at[0], sibling).wait_send()

    barrier = pltpu.get_barrier_semaphore()
    target_peers = [z_partner, query_partner, device(query_x, y, pair_z, core)]
    row_peers = [(d, other) for d in range(NX) for other in (False, True) if d or other]
    greeted = [ring_device(way, column) for way in (1, -1) for column in (None, key_x)] + [z_partner, target_peers[2]]
    greeted += [y_device(d) for d in range(1, NY)] + [row_device(*p) for p in row_peers]
    for other in greeted:
        pl.semaphore_signal(barrier, inc=1, device_id=other, device_id_type=MESH)

    loads = [
        pltpu.make_async_copy(futures_hbm, futures, in_sem.at[0]),
        pltpu.make_async_copy(segments_hbm, segments, in_sem.at[1]),
        pltpu.make_async_copy(pairs_hbm, pairs, in_sem.at[2]),
    ]
    for load in loads:
        load.start()

    def column(combo):
        w = 1 - odd_z if combo in (1, 3) else odd_z
        v = 1 - odd_x if combo in (2, 3) else odd_x
        return w * 2 + v

    def query_slot(combo, offset, c):
        return column(combo) * 8 + lax.rem(y - offset + NY, NY) * 2 + c

    loads[0].wait()
    key_unit, key_inverse = unit_rows(futures[...])
    keys[0] = key_unit
    loads[1].wait()
    query_unit, query_inverse = unit_rows(segments[...])
    queries[query_slot(0, 0, core)] = query_unit
    loads[2].wait()
    mine = pairs[...]
    parts = [
        jnp.where(x // 2 == 0, mine[:, 64 * i : 64 * i + 32], mine[:, 64 * i + 32 : 64 * i + 64]) for i in range(NY)
    ]
    targets[column(0)] = jnp.concatenate(parts, axis=1)
    pl.semaphore_wait(barrier, len(greeted))

    def half_rows(half):
        return pl.ds(half * HALF, HALF)

    def gather_ring(way, step, half):
        rows = half_rows(half)
        return remote(
            keys.at[2 * place_of(way, step - 1), rows], keys.at[2 * place_of(way, step), rows],
            KZ, kz_recv.at[way, step - 1, half], ring_device(1 if way == 0 else -1),
        )

    def gather_far(way):
        rows = half_rows(way)
        return remote(
            keys.at[2 * place_of(way, FAR - 1), rows], keys.at[2 * RING - 1, rows],
            KZ, kx_recv.at[RING - 1], ring_device(1 if way == 0 else -1, key_x),
        )

    def gather_x(place):
        return remote(keys.at[2 * place], keys.at[2 * place + 1], KX, kx_recv.at[place], key_partner)

    def step_ring(step):
        for half in range(HALVES):
            for way in range(2):
                if step > 0 and has(way, step, half):
                    gather_ring(way, step, half).wait_recv()
                if step < FAR and has(way, step + 1, half):
                    gather_ring(way, step + 1, half).start()
                    if step + 1 == FAR:
                        gather_far(way).start()
        if step < FAR:
            for way in range(2):
                if step > 0 or way == 0:
                    gather_x(place_of(way, step)).start()

    def await_x(place):
        await_recv(keys.at[2 * place + 1], KX, kx_recv.at[place])

    def gather_partner(combo):
        slot = queries.at[query_slot(0 if combo < 3 else 1, 0, core)]
        return remote(slot, slot, QP, qp_recv.at[combo], z_partner if combo == 1 else query_partner)

    def gather_y(combo, offset):
        slot = queries.at[query_slot(combo, 0, core)]
        return remote(slot, slot, QY, qy_recv.at[combo], y_device(offset))

    def gather_sibling(combo, offset):
        slot = queries.at[query_slot(combo, offset, core)]
        return remote(slot, slot, QS, qs_recv.at[combo], sibling)

    def split_query(slot):
        high, low = split(queries[slot])
        rows = pl.ds(pl.multiple_of(slot * ROWS, ROWS), ROWS)
        queries_high[rows] = high
        queries_low[rows] = low

    def split_keys(first, last):
        high, low = split(keys[first:last].reshape((last - first) * ROWS, WIDTH))
        keys_high[first * ROWS : last * ROWS] = high
        keys_low[first * ROWS : last * ROWS] = low

    def spread(combo):
        if combo > 0:
            gather_partner(combo).wait_recv()
        if combo == 1:
            gather_partner(3).start()
        for offset in (2, 1, 3):
            gather_y(combo, offset).start()
        gather_sibling(combo, 0).start()
        split_query(query_slot(combo, 0, core))

    def take_y(combo):
        await_recv(queries.at[pl.ds(0, 3)], QY, qy_recv.at[combo])
        for offset in (1, 3, 2):
            gather_sibling(combo, offset).start()
        for offset in (1, 3, 2):
            split_query(query_slot(combo, offset, core))

    def take_sibling(combo):
        await_recv(queries.at[pl.ds(0, 4)], QS, qs_recv.at[combo])
        for offset in (0, 1, 3, 2):
            split_query(query_slot(combo, offset, 1 - core))

    step_ring(0)
    gather_partner(1).start()
    gather_partner(2).start()
    spread(0)
    mine_target = targets.at[column(0)]
    for to in target_peers:
        remote(mine_target, mine_target, TG, once_recv.at[0], to).start()
    scale = jnp.exp(log_scale[...])
    bias = logit_bias[...]
    spread(1)
    spread(2)
    step_ring(1)
    take_y(0)
    spread(3)
    step_ring(2)
    take_y(1)
    take_sibling(0)
    take_y(2)
    step_ring(3)
    take_sibling(1)
    take_y(3)
    take_sibling(2)
    take_sibling(3)
    await_recv(targets.at[pl.ds(0, 3)], TG, once_recv.at[0])

    def pair_block(first, last):
        a, b = first * ROWS, last * ROWS
        raw = dot3(
            keys_high[a:b], keys_low[a:b], queries_high[...], queries_low[...], NT
        )
        value = scale * raw + bias
        row = lax.broadcasted_iota(jnp.int32, (b - a, 1), 0) + a
        place = row // (2 * ROWS)
        step = (place + 1) // 2
        line = lax.rem(z + 2 * jnp.where(place % 2 == 1, RING - step, step), NZ)
        low_x = jnp.where(row // ROWS % 2 == 1, 1 - odd_x, odd_x)
        key_row = (low_x * NZ + line) * (ROWS * 16) + lax.axis_index("ka") * ROWS + row % ROWS
        target = jnp.concatenate([targets[i] for i in range(4)], axis=1)
        hit = key_row == target
        small = jnp.exp(-jnp.abs(value))
        sigmoid = jnp.where(value >= 0, f32(1.0), small) / (f32(1.0) + small)
        weight = sigmoid - hit.astype(f32)
        softplus = jnp.maximum(value, f32(0.0)) + jnp.log1p(small)
        weights[a:b] = scale * weight
        loss = fold(softplus - jnp.where(hit, value, f32(0.0)))
        by_scale = fold(weight * (value - bias))
        by_bias = fold(weight)
        return jnp.concatenate([loss, by_scale, by_bias, jnp.zeros((5, 128), f32)], axis=0)

    def key_block(first, last):
        a, b = first * ROWS, last * ROWS
        high, low = split(weights[a:b])
        out = dot3(high, low, queries_high[...], queries_low[...], NN)
        key_terms[first:last] = out.reshape(last - first, ROWS, WIDTH)

    for place in range(FIRST // 2):
        await_x(place)
    split_keys(0, FIRST)
    totals = pair_block(0, FIRST)
    step_ring(4)
    for place in range(FIRST // 2, RING):
        await_x(place)
    split_keys(FIRST, CHIPS)
    totals = totals + pair_block(FIRST, CHIPS)
    key_block(FIRST, CHIPS)

    def sum_x(place):
        return remote(key_terms.at[2 * place + 1], x_terms.at[place], RX, rx_recv.at[place], key_partner)

    def sum_far(way):
        rows = half_rows(way)
        return remote(
            key_terms.at[2 * RING - 1, rows], x_terms.at[RING - 1, rows],
            RX, rx_recv.at[RING - 1 + way], ring_device(-1 if way == 0 else 1, key_x),
        )

    def sum_ring(way, step, half):
        rows = half_rows(half)
        return remote(
            key_terms.at[2 * place_of(way, step), rows], ring_terms.at[way, step - 1, rows],
            RZ, rz_recv.at[way, step - 1, half], ring_device(-1 if way == 0 else 1),
        )

    def start_x(*places):
        for place in places:
            sum_x(place).start()

    def start_far():
        for way in range(2):
            sum_ring(way, FAR, way).start()
            sum_far(way).start()

    def reduce_ring(step):
        for half in range(HALVES):
            rows = half_rows(half)
            for way in range(2):
                place = place_of(way, step)
                if half == 0:
                    sum_x(place).wait_recv()
                total = key_terms[2 * place, rows] + x_terms[place, rows]
                if has(way, step + 1, half):
                    sum_ring(way, step + 1, half).wait_recv()
                    total = total + ring_terms[way, step, rows]
                if step + 1 == FAR and way == half:
                    sum_far(way).wait_recv()
                    total = total + x_terms[RING - 1, rows]
                key_terms[2 * place, rows] = total
                sum_ring(way, step, half).start()

    start_far()
    start_x(5, 6)

    def start_line():
        slot = sums_line.at[z // 2]
        sums_line[z // 2] = totals
        for d in range(1, RING):
            remote(slot, slot, SL, once_recv.at[1], ring_device(d)).start()

    def start_two():
        await_recv(sums_line.at[pl.ds(0, RING - 1)], SL, once_recv.at[1])
        sums_two[odd_z] = jnp.sum(sums_line[...], axis=0)
        slot = sums_two.at[odd_z]
        remote(slot, slot, SW, once_recv.at[2], z_partner).start()

    def start_row():
        await_recv(sums_two.at[0], SW, once_recv.at[2])
        sums_row[x * 2 + core] = sums_two[0] + sums_two[1]
        slot = sums_row.at[x * 2 + core]
        for p in row_peers:
            remote(slot, slot, SR, once_recv.at[3], row_device(*p)).start()

    def start_column():
        await_recv(sums_row.at[pl.ds(0, 2 * NX - 1)], SR, once_recv.at[3])
        sums_y[y] = jnp.sum(sums_row[...], axis=0)
        slot = sums_y.at[y]
        for d in range(1, NY):
            remote(slot, slot, SY, once_recv.at[4], y_device(d)).start()

    def finish_scalars():
        await_recv(sums_y.at[pl.ds(0, NY - 1)], SY, once_recv.at[4])
        total = jnp.sum(sums_y[...], axis=0) * f32(1.0 / 8192)
        scalars[...] = jnp.broadcast_to(jnp.sum(total, axis=1, keepdims=True), scalars.shape)

    def query_block(combo):
        rows = pl.ds(pl.multiple_of(column(combo) * 8 * ROWS, 8 * ROWS), 8 * ROWS)
        out = dot3(weights_high[rows], weights_low[rows], keys_high[...], keys_low[...], NN)
        query_terms[combo] = out.reshape(NY, 2, ROWS, WIDTH)
        for place in range(NY):
            remote(
                query_terms.at[combo, place, 1 - core], sibling_terms.at[combo, place],
                RS, rs_recv.at[combo], sibling,
            ).start()

    def sum_y(combo, offset):
        return remote(
            query_terms.at[combo, lax.rem(y + offset, NY), core], y_terms.at[combo, offset],
            RY, ry_recv.at[combo], y_device(offset),
        )

    def start_y(combo):
        await_recv(sibling_terms.at[combo], RS, rs_recv.at[combo])
        for offset in (2, 1, 3, 0):
            place = lax.rem(y + offset, NY)
            query_terms[combo, place, core] = query_terms[combo, place, core] + sibling_terms[combo, place]
            if offset > 0:
                sum_y(combo, offset).start()

    def take_column(combo):
        await_recv(y_terms.at[combo, pl.ds(1, 3)], RY, ry_recv.at[combo])
        return ((y_terms[combo, 1] + y_terms[combo, 3]) + y_terms[combo, 2]) + query_terms[combo, y, core]

    def sum_partner(combo):
        return remote(
            pair_terms.at[combo], z_terms.at[combo], RP, rp_recv.at[combo],
            z_partner if combo == 1 else query_partner,
        )

    start_line()
    high, low = split(weights[...].T)
    weights_high[...] = high
    weights_low[...] = low
    query_block(3)
    query_block(2)
    start_y(3)
    query_block(1)
    start_y(2)
    query_block(0)
    start_y(1)
    reduce_ring(3)
    key_block(0, FIRST)
    start_x(3, 4, 1, 2, 0)
    start_y(0)
    start_two()
    reduce_ring(2)
    for combo in (3, 2):
        pair_terms[combo] = take_column(combo)
        sum_partner(combo).start()
    start_row()
    near = take_column(1)
    sum_partner(3).wait_recv()
    pair_terms[1] = near + z_terms[3]
    sum_partner(1).start()
    reduce_ring(1)
    start_column()

    query_grad = take_column(0)
    sum_partner(2).wait_recv()
    query_grad = query_grad + z_terms[2]
    sum_partner(1).wait_recv()
    query_grad = query_grad + z_terms[1]
    grad_segments[...] = backward(query_unit, query_grad, query_inverse)

    finish_scalars()

    sum_x(0).wait_recv()
    for half in range(HALVES):
        for way in range(2):
            sum_ring(way, 1, half).wait_recv()
    key_grad = (key_terms[0] + x_terms[0]) + (ring_terms[0, 0] + ring_terms[1, 0])
    grad_futures[...] = backward(key_unit, key_grad, key_inverse)

    def blocks(ref, count):
        return ref.at[pl.ds(0, count)]

    await_send(blocks(keys, 8), KZ)
    await_send(blocks(keys, 7), KX)
    await_send(blocks(queries, 3), QP)
    await_send(blocks(queries, 12), QY)
    await_send(blocks(queries, 16), QS)
    await_send(blocks(targets, 3), TG)
    await_send(blocks(key_terms, 8), RX)
    await_send(blocks(key_terms, 7), RZ)
    await_send(blocks(queries, 16), RS)
    await_send(blocks(queries, 12), RY)
    await_send(blocks(queries, 3), RP)
    await_send(blocks(sums_line, RING - 1), SL)
    await_send(sums_two.at[0], SW)
    await_send(blocks(sums_row, 2 * NX - 1), SR)
    await_send(blocks(sums_y, NY - 1), SY)


def per_device(segments, futures, pair_index, log_scale, logit_bias):
    dma = pltpu.SemaphoreType.DMA
    vmem = pltpu.VMEM
    block = (ROWS, WIDTH)
    sums = (8, 128)
    in_vmem = pl.BlockSpec(memory_space=pltpu.VMEM)
    in_hbm = pl.BlockSpec(memory_space=pltpu.HBM)

    grad_segments, grad_futures, scalars = pl.pallas_call(
        kernel,
        out_shape=(
            jax.ShapeDtypeStruct(block, f32),
            jax.ShapeDtypeStruct(block, f32),
            jax.ShapeDtypeStruct(sums, f32),
        ),
        in_specs=[in_hbm] * 3 + [in_vmem] * 2,
        out_specs=(in_vmem, in_vmem, in_vmem),
        scratch_shapes=[
            vmem(block, f32),
            vmem(block, f32),
            vmem((1, 256), jnp.int32),
            vmem((CHIPS * 2,) + block, f32),
            vmem((QUERIES, WIDTH), bf16),
            vmem((QUERIES, WIDTH), bf16),
            vmem((CHIPS,) + block, f32),
            vmem((KEYS, WIDTH), bf16),
            vmem((KEYS, WIDTH), bf16),
            vmem((KEYS, QUERIES), f32),
            vmem((QUERIES, KEYS), bf16),
            vmem((QUERIES, KEYS), bf16),
            vmem((CHIPS,) + block, f32),
            vmem((RING,) + block, f32),
            vmem((2, FAR) + block, f32),
            vmem((4, NY, 2) + block, f32),
            vmem((4, NY) + block, f32),
            vmem((4, NY) + block, f32),
            vmem((4,) + block, f32),
            vmem((4,) + block, f32),
            vmem((4, 1, 128), jnp.int32),
            vmem((RING,) + sums, f32),
            vmem((2,) + sums, f32),
            vmem((2 * NX,) + sums, f32),
            vmem((NY,) + sums, f32),
            dma((3,)),
            dma((15,)),
            dma((2, FAR, HALVES)),
            dma((RING,)),
            dma((4,)),
            dma((4,)),
            dma((4,)),
            dma((RING + 1,)),
            dma((2, FAR, HALVES)),
            dma((4,)),
            dma((4,)),
            dma((4,)),
            dma((5,)),
        ],
        compiler_params=pltpu.CompilerParams(
            collective_id=0, has_side_effects=True, vmem_limit_bytes=40 << 20
        ),
    )(
        segments,
        futures,
        pair_index.reshape(1, 256),
        log_scale.reshape(1, 1),
        logit_bias.reshape(1, 1),
    )
    return grad_segments, grad_futures, scalars[:3, 0]


def solution(mesh):
    in_specs = (P(("pb", "ka"), None), P(("pb", "ka"), None), P("pb"), P(), P())
    out_specs = (P(("pb", "ka"), None), P(("pb", "ka"), None), P())
    return jax.shard_map(
        per_device, mesh=mesh, in_specs=in_specs, out_specs=out_specs, check_vma=False
    )
```

```python
import jax
import jax.numpy as jnp
from jax import lax
from jax.experimental import pallas as pl
from jax.experimental.pallas import tpu as pltpu
from jax.sharding import PartitionSpec as P

MESH = pl.DeviceIdType.MESH
f32 = jnp.float32
bf16 = jnp.bfloat16
epsilon = 1e-06

NX, NY, NZ = 4, 4, 16
RING = 8
ROWS = 16
WIDTH = 1024
CHIPS = 16
QUERIES = CHIPS * 2 * ROWS
KEYS = CHIPS * ROWS
FIRST = 10
HALVES = 2
HALF = ROWS // HALVES
FAR = 7
KZ, KX, QP, QY, QS, TG, RX, RZ, RS, RY, RP, SG, SA = range(13)


def coordinates():
    pb = lax.axis_index("pb")
    ka = lax.axis_index("ka")
    return lax.rem(ka // 2, 2) * 2 + pb // NZ, ka // 4, lax.rem(pb, NZ), lax.rem(ka, 2)


def device(x, y, z, core):
    return (lax.rem(x, 2) * NZ + z, y * 4 + (x // 2) * 2 + core)


def split(value):
    high = value.astype(bf16)
    return high, (value - high.astype(f32)).astype(bf16)


def dot(a, b, dims):
    return lax.dot_general(a, b, (dims, ((), ())), preferred_element_type=f32)


def dot3(a_high, a_low, b_high, b_low, dims):
    return (dot(a_low, b_high, dims) + dot(a_high, b_low, dims)) + dot(a_high, b_high, dims)


NN = ((1,), (0,))
NT = ((1,), (1,))


def fold(value):
    rows = jnp.sum(value, axis=0, keepdims=True)
    return rows[:, 0:128] + rows[:, 128:256] + rows[:, 256:384] + rows[:, 384:512]


def unit_rows(value):
    inverse = lax.rsqrt(jnp.sum(value * value, axis=1, keepdims=True) + epsilon)
    return value * inverse, inverse


def backward(direction, grad, inverse):
    return (grad - direction * jnp.sum(direction * grad, axis=1, keepdims=True)) * inverse


def kernel(
    segments_hbm, futures_hbm, pairs_hbm, log_scale, logit_bias,
    segments_out, futures_out, scalars_out,
    segments, futures, pairs, grad_segments, grad_futures, scalars,
    queries, queries_high, queries_low, keys, keys_high, keys_low,
    weights, weights_high, weights_low, key_terms, x_terms, line_terms,
    query_terms, sibling_terms, y_terms, pair_terms, z_terms, targets,
    sums_group, sums_all,
    in_sem, out_sem, send, kz_recv, kx_recv, qp_recv, qy_recv, qs_recv,
    rx_recv, rz_recv, rs_recv, ry_recv, rp_recv, once_recv,
):
    x, y, z, core = coordinates()
    odd_x, odd_z = lax.rem(x, 2), lax.rem(z, 2)
    sign = 1 - 2 * odd_z
    key_x = x + 1 - 2 * odd_x
    query_x = lax.rem(x + 2 * odd_x + NX - 1, NX)
    pair_z = z + 1 - 2 * odd_z

    sibling = device(x, y, z, 1 - core)
    key_partner = device(key_x, y, z, core)
    query_partner = device(query_x, y, z, core)
    z_partner = device(x, y, pair_z, core)

    def y_device(offset):
        return device(x, lax.rem(y + offset, NY), z, core)

    def line_device(distance, column=None):
        return device(x if column is None else column, y, lax.rem(z + sign * distance + NZ, NZ), core)

    def row_device(offset, other):
        return device(lax.rem(x + offset, NX), y, z, 1 - core if other else core)

    def remote(src, dst, kind, recv, to):
        return pltpu.make_async_remote_copy(
            src_ref=src, dst_ref=dst, send_sem=send.at[kind], recv_sem=recv, device_id=to, device_id_type=MESH
        )

    def await_recv(ref, kind, recv):
        remote(ref, ref, kind, recv, sibling).wait_recv()

    def await_send(ref, kind):
        remote(ref, ref, kind, once_recv.at[0], sibling).wait_send()

    barrier = pltpu.get_barrier_semaphore()
    target_peers = [z_partner, query_partner, device(query_x, y, pair_z, core)]
    row_peers = [(d, other) for d in range(NX) for other in (False, True) if d or other]
    greeted = [line_device(d, column) for d in (2, -2) for column in (None, key_x)]
    greeted += [line_device(-1), z_partner, target_peers[2]]
    greeted += [y_device(d) for d in range(1, NY)] + [row_device(*p) for p in row_peers]
    for other in greeted:
        pl.semaphore_signal(barrier, inc=1, device_id=other, device_id_type=MESH)

    loads = [
        pltpu.make_async_copy(futures_hbm, futures, in_sem.at[0]),
        pltpu.make_async_copy(segments_hbm, segments, in_sem.at[1]),
        pltpu.make_async_copy(pairs_hbm, pairs, in_sem.at[2]),
    ]
    for load in loads:
        load.start()

    def column(combo):
        w = 1 - odd_z if combo in (1, 3) else odd_z
        v = 1 - odd_x if combo in (2, 3) else odd_x
        return w * 2 + v

    def query_slot(combo, offset, c):
        return column(combo) * 8 + lax.rem(y - offset + NY, NY) * 2 + c

    loads[0].wait()
    key_unit, key_inverse = unit_rows(futures[...])
    keys[0] = key_unit
    loads[1].wait()
    query_unit, query_inverse = unit_rows(segments[...])
    queries[query_slot(0, 0, core)] = query_unit
    loads[2].wait()
    mine = pairs[...]
    parts = [
        jnp.where(x // 2 == 0, mine[:, 64 * i : 64 * i + 32], mine[:, 64 * i + 32 : 64 * i + 64]) for i in range(NY)
    ]
    targets[column(0)] = jnp.concatenate(parts, axis=1)
    pl.semaphore_wait(barrier, len(greeted))

    def half_rows(half):
        return pl.ds(half * HALF, HALF)

    def gather_line(place, half):
        rows = half_rows(half)
        return remote(
            keys.at[2 * max(place - 2, 0), rows], keys.at[2 * place, rows],
            KZ, kz_recv.at[place - 1, half], line_device(-1 if place == 1 else 2),
        )

    def gather_far(half):
        rows = half_rows(half)
        return remote(
            keys.at[2 * (FAR - 2), rows], keys.at[2 * FAR + 1, rows], KZ, kx_recv.at[FAR], line_device(2, key_x)
        )

    def gather_x(place):
        return remote(keys.at[2 * place], keys.at[2 * place + 1], KX, kx_recv.at[place], key_partner)

    def step_line(*places):
        for place in places:
            for half in range(HALVES):
                gather_line(place, half).wait_recv()
                if place + 2 <= FAR:
                    gather_line(place + 2, half).start()
                if place + 2 == FAR:
                    gather_far(half).start()
        for place in places:
            if place < FAR:
                gather_x(place).start()

    def await_x(place):
        await_recv(keys.at[2 * place + 1], KX, kx_recv.at[place])

    def gather_partner(combo):
        slot = queries.at[query_slot(0 if combo < 3 else 1, 0, core)]
        return remote(slot, slot, QP, qp_recv.at[combo], z_partner if combo == 1 else query_partner)

    def gather_y(combo, offset):
        slot = queries.at[query_slot(combo, 0, core)]
        return remote(slot, slot, QY, qy_recv.at[combo], y_device(offset))

    def gather_sibling(combo, offset):
        slot = queries.at[query_slot(combo, offset, core)]
        return remote(slot, slot, QS, qs_recv.at[combo], sibling)

    def split_query(slot):
        high, low = split(queries[slot])
        rows = pl.ds(pl.multiple_of(slot * ROWS, ROWS), ROWS)
        queries_high[rows] = high
        queries_low[rows] = low

    def split_keys(first, last):
        high, low = split(keys[first:last].reshape((last - first) * ROWS, WIDTH))
        keys_high[first * ROWS : last * ROWS] = high
        keys_low[first * ROWS : last * ROWS] = low

    def spread(combo):
        if combo > 0:
            gather_partner(combo).wait_recv()
        if combo == 1:
            gather_partner(3).start()
        for offset in (2, 1, 3):
            gather_y(combo, offset).start()
        gather_sibling(combo, 0).start()
        split_query(query_slot(combo, 0, core))

    def take_y(combo):
        await_recv(queries.at[pl.ds(0, 3)], QY, qy_recv.at[combo])
        for offset in (1, 3, 2):
            gather_sibling(combo, offset).start()
        for offset in (1, 3, 2):
            split_query(query_slot(combo, offset, core))

    def take_sibling(combo):
        await_recv(queries.at[pl.ds(0, 4)], QS, qs_recv.at[combo])
        for offset in (0, 1, 3, 2):
            split_query(query_slot(combo, offset, 1 - core))

    for half in range(HALVES):
        gather_line(1, half).start()
        gather_line(2, half).start()
    gather_x(0).start()
    gather_partner(1).start()
    gather_partner(2).start()
    spread(0)
    mine_target = targets.at[column(0)]
    for to in target_peers:
        remote(mine_target, mine_target, TG, once_recv.at[0], to).start()
    scale = jnp.exp(log_scale[...])
    bias = logit_bias[...]
    spread(1)
    spread(2)
    step_line(1, 2)
    take_y(0)
    spread(3)
    step_line(3, 4)
    take_y(1)
    take_sibling(0)
    take_y(2)
    step_line(5, 6)
    take_sibling(1)
    take_y(3)
    take_sibling(2)
    take_sibling(3)
    await_recv(targets.at[pl.ds(0, 3)], TG, once_recv.at[0])

    def pair_block(first, last):
        a, b = first * ROWS, last * ROWS
        raw = dot3(
            keys_high[a:b], keys_low[a:b], queries_high[...], queries_low[...], NT
        )
        value = scale * raw + bias
        row = lax.broadcasted_iota(jnp.int32, (b - a, 1), 0) + a
        place = row // (2 * ROWS)
        line = lax.rem(z + NZ - sign * place, NZ)
        low_x = jnp.where(row // ROWS % 2 == 1, 1 - odd_x, odd_x)
        key_row = (low_x * NZ + line) * (ROWS * 16) + lax.axis_index("ka") * ROWS + row % ROWS
        target = jnp.concatenate([targets[i] for i in range(4)], axis=1)
        hit = key_row == target
        small = jnp.exp(-jnp.abs(value))
        sigmoid = jnp.where(value >= 0, f32(1.0), small) / (f32(1.0) + small)
        weight = sigmoid - hit.astype(f32)
        softplus = jnp.maximum(value, f32(0.0)) + jnp.log1p(small)
        weights[a:b] = scale * weight
        loss = fold(softplus - jnp.where(hit, value, f32(0.0)))
        by_scale = fold(weight * (value - bias))
        by_bias = fold(weight)
        return jnp.concatenate([loss, by_scale, by_bias, jnp.zeros((5, 128), f32)], axis=0)

    def key_block(first, last):
        a, b = first * ROWS, last * ROWS
        high, low = split(weights[a:b])
        out = dot3(high, low, queries_high[...], queries_low[...], NN)
        key_terms[first:last] = out.reshape(last - first, ROWS, WIDTH)

    for place in range(FIRST // 2):
        await_x(place)
    split_keys(0, FIRST)
    totals = pair_block(0, FIRST)
    step_line(7)
    for place in range(FIRST // 2, RING):
        await_x(place)
    split_keys(FIRST, CHIPS)
    totals = totals + pair_block(FIRST, CHIPS)

    def start_group():
        place = column(0) * 8 + y * 2 + core
        sums_group[place] = totals
        slot = sums_group.at[place]
        for i in range(1, 2 * CHIPS):
            far_x, far_z = query_x if i // 8 % 2 else x, pair_z if i // 16 else z
            to = device(far_x, lax.rem(y + i // 2, NY), far_z, lax.rem(core + i, 2))
            remote(slot, slot, SG, once_recv.at[1], to).start()

    start_group()
    key_block(FIRST, CHIPS)

    def sum_x(place):
        return remote(key_terms.at[2 * place + 1], x_terms.at[place], RX, rx_recv.at[place], key_partner)

    def sum_far(half):
        rows = half_rows(half)
        return remote(
            key_terms.at[2 * FAR + 1, rows], x_terms.at[FAR, rows], RX, rx_recv.at[FAR + half], line_device(-2, key_x)
        )

    def sum_line(place, half):
        rows = half_rows(half)
        return remote(
            key_terms.at[2 * place, rows], line_terms.at[place - 1, rows],
            RZ, rz_recv.at[place - 1, half], line_device(-1 if place == 1 else -2),
        )

    def start_x(*places):
        for place in places:
            sum_x(place).start()

    def start_far():
        for half in range(HALVES):
            sum_line(FAR, half).start()
            sum_far(half).start()

    def reduce_line(place):
        sum_x(place).wait_recv()
        for half in range(HALVES):
            rows = half_rows(half)
            total = key_terms[2 * place, rows] + x_terms[place, rows]
            if place + 2 <= FAR:
                sum_line(place + 2, half).wait_recv()
                total = total + line_terms[place + 1, rows]
            if place + 2 == FAR:
                sum_far(half).wait_recv()
                total = total + x_terms[FAR, rows]
            key_terms[2 * place, rows] = total
            sum_line(place, half).start()

    start_far()
    start_x(5, 6)

    def start_all():
        await_recv(sums_group.at[pl.ds(0, 2 * CHIPS - 1)], SG, once_recv.at[1])
        place = z // 2 * 2 + lax.rem((x + 1) // 2, 2)
        sums_all[place] = jnp.sum(sums_group[...], axis=0)
        slot = sums_all.at[place]
        for d in range(RING):
            if d > 0:
                remote(slot, slot, SA, once_recv.at[2], line_device(-d)).start()
            remote(slot, slot, SA, once_recv.at[2], line_device(-d, key_x)).start()

    def finish_scalars():
        await_recv(sums_all.at[pl.ds(0, CHIPS - 1)], SA, once_recv.at[2])
        total = jnp.sum(sums_all[...], axis=0) * f32(1.0 / 8192)
        for i in range(3):
            scalars[i] = jnp.sum(total[i : i + 1, :])

    def query_block(combo):
        rows = pl.ds(pl.multiple_of(column(combo) * 8 * ROWS, 8 * ROWS), 8 * ROWS)
        out = dot3(weights_high[rows], weights_low[rows], keys_high[...], keys_low[...], NN)
        query_terms[combo] = out.reshape(NY, 2, ROWS, WIDTH)
        for place in range(NY):
            remote(
                query_terms.at[combo, place, 1 - core], sibling_terms.at[combo, place],
                RS, rs_recv.at[combo], sibling,
            ).start()

    def sum_y(combo, offset):
        return remote(
            query_terms.at[combo, lax.rem(y + offset, NY), core], y_terms.at[combo, offset],
            RY, ry_recv.at[combo], y_device(offset),
        )

    def start_y(combo):
        await_recv(sibling_terms.at[combo], RS, rs_recv.at[combo])
        for offset in (2, 1, 3, 0):
            place = lax.rem(y + offset, NY)
            query_terms[combo, place, core] = query_terms[combo, place, core] + sibling_terms[combo, place]
            if offset > 0:
                sum_y(combo, offset).start()

    def take_column(combo):
        await_recv(y_terms.at[combo, pl.ds(1, 3)], RY, ry_recv.at[combo])
        return ((y_terms[combo, 1] + y_terms[combo, 3]) + y_terms[combo, 2]) + query_terms[combo, y, core]

    def sum_partner(combo):
        return remote(
            pair_terms.at[combo], z_terms.at[combo], RP, rp_recv.at[combo],
            z_partner if combo == 1 else query_partner,
        )

    high, low = split(weights[...].T)
    weights_high[...] = high
    weights_low[...] = low
    query_block(3)
    query_block(2)
    start_y(3)
    query_block(1)
    start_y(2)
    query_block(0)
    start_y(1)
    reduce_line(6)
    reduce_line(5)
    key_block(0, FIRST)
    start_x(3, 4, 1, 2, 0)
    start_y(0)
    start_all()
    reduce_line(3)
    reduce_line(4)
    for combo in (3, 2):
        pair_terms[combo] = take_column(combo)
        sum_partner(combo).start()
    near = take_column(1)
    sum_partner(3).wait_recv()
    pair_terms[1] = near + z_terms[3]
    sum_partner(1).start()
    reduce_line(1)
    reduce_line(2)

    query_grad = take_column(0)
    sum_partner(2).wait_recv()
    query_grad = query_grad + z_terms[2]
    sum_partner(1).wait_recv()
    query_grad = query_grad + z_terms[1]
    grad_segments[...] = backward(query_unit, query_grad, query_inverse)
    stores = [
        pltpu.make_async_copy(grad_segments, segments_out, out_sem.at[0]),
        pltpu.make_async_copy(scalars, scalars_out, out_sem.at[1]),
        pltpu.make_async_copy(grad_futures, futures_out, out_sem.at[2]),
    ]
    stores[0].start()

    finish_scalars()
    stores[1].start()

    sum_x(0).wait_recv()
    for half in range(HALVES):
        sum_line(1, half).wait_recv()
        sum_line(2, half).wait_recv()
    key_grad = (key_terms[0] + x_terms[0]) + (line_terms[0] + line_terms[1])
    grad_futures[...] = backward(key_unit, key_grad, key_inverse)
    stores[2].start()

    def blocks(ref, count):
        return ref.at[pl.ds(0, count)]

    await_send(blocks(keys, 8), KZ)
    await_send(blocks(keys, 7), KX)
    await_send(blocks(queries, 3), QP)
    await_send(blocks(queries, 12), QY)
    await_send(blocks(queries, 16), QS)
    await_send(blocks(targets, 3), TG)
    await_send(blocks(key_terms, 8), RX)
    await_send(blocks(key_terms, 7), RZ)
    await_send(blocks(queries, 16), RS)
    await_send(blocks(queries, 12), RY)
    await_send(blocks(queries, 3), RP)
    await_send(blocks(sums_group, 2 * CHIPS - 1), SG)
    await_send(blocks(sums_all, CHIPS - 1), SA)
    for store in stores:
        store.wait()


def per_device(segments, futures, pair_index, log_scale, logit_bias):
    dma = pltpu.SemaphoreType.DMA
    vmem = pltpu.VMEM
    block = (ROWS, WIDTH)
    sums = (8, 128)
    in_vmem = pl.BlockSpec(memory_space=pltpu.VMEM)
    in_hbm = pl.BlockSpec(memory_space=pltpu.HBM)

    grad_segments, grad_futures, scalars = pl.pallas_call(
        kernel,
        out_shape=(
            jax.ShapeDtypeStruct(block, f32),
            jax.ShapeDtypeStruct(block, f32),
            jax.ShapeDtypeStruct((3,), f32),
        ),
        in_specs=[in_hbm] * 3 + [in_vmem] * 2,
        out_specs=(in_hbm,) * 3,
        scratch_shapes=[
            vmem(block, f32),
            vmem(block, f32),
            vmem((1, 256), jnp.int32),
            vmem(block, f32),
            vmem(block, f32),
            pltpu.SMEM((3,), f32),
            vmem((CHIPS * 2,) + block, f32),
            vmem((QUERIES, WIDTH), bf16),
            vmem((QUERIES, WIDTH), bf16),
            vmem((CHIPS,) + block, f32),
            vmem((KEYS, WIDTH), bf16),
            vmem((KEYS, WIDTH), bf16),
            vmem((KEYS, QUERIES), f32),
            vmem((QUERIES, KEYS), bf16),
            vmem((QUERIES, KEYS), bf16),
            vmem((CHIPS,) + block, f32),
            vmem((RING,) + block, f32),
            vmem((FAR,) + block, f32),
            vmem((4, NY, 2) + block, f32),
            vmem((4, NY) + block, f32),
            vmem((4, NY) + block, f32),
            vmem((4,) + block, f32),
            vmem((4,) + block, f32),
            vmem((4, 1, 128), jnp.int32),
            vmem((2 * CHIPS,) + sums, f32),
            vmem((CHIPS,) + sums, f32),
            dma((3,)),
            dma((3,)),
            dma((13,)),
            dma((FAR, HALVES)),
            dma((RING,)),
            dma((4,)),
            dma((4,)),
            dma((4,)),
            dma((RING + 1,)),
            dma((FAR, HALVES)),
            dma((4,)),
            dma((4,)),
            dma((4,)),
            dma((3,)),
        ],
        compiler_params=pltpu.CompilerParams(
            collective_id=0, has_side_effects=True, vmem_limit_bytes=62 << 20
        ),
    )(
        segments,
        futures,
        pair_index.reshape(1, 256),
        log_scale.reshape(1, 1),
        logit_bias.reshape(1, 1),
    )
    return grad_segments, grad_futures, scalars


def solution(mesh):
    in_specs = (P(("pb", "ka"), None), P(("pb", "ka"), None), P("pb"), P(), P())
    out_specs = (P(("pb", "ka"), None), P(("pb", "ka"), None), P())
    return jax.shard_map(
        per_device, mesh=mesh, in_specs=in_specs, out_specs=out_specs, check_vma=False
    )
```

```python
import jax
import jax.numpy as jnp
from jax import lax
from jax.experimental import pallas as pl
from jax.experimental.pallas import tpu as pltpu
from jax.sharding import PartitionSpec as P

MESH = pl.DeviceIdType.MESH
f32 = jnp.float32
bf16 = jnp.bfloat16
epsilon = 1e-06

NX, NY, NZ = 4, 4, 16
RING = 8
ROWS = 16
WIDTH = 1024
CHIPS = 16
QUERIES = CHIPS * 2 * ROWS
KEYS = CHIPS * ROWS
FIRST = 10
HALVES = 2
HALF = ROWS // HALVES
FAR = 7
KZ, KX, QP, QY, QS, TG, RX, RZ, RS, RY, RP, SG, SA = range(13)


def coordinates():
    pb = lax.axis_index("pb")
    ka = lax.axis_index("ka")
    return lax.rem(ka // 2, 2) * 2 + pb // NZ, ka // 4, lax.rem(pb, NZ), lax.rem(ka, 2)


def device(x, y, z, core):
    return (lax.rem(x, 2) * NZ + z, y * 4 + (x // 2) * 2 + core)


def split(value):
    high = value.astype(bf16)
    return high, (value - high.astype(f32)).astype(bf16)


def dot(a, b, dims):
    return lax.dot_general(a, b, (dims, ((), ())), preferred_element_type=f32)


def dot3(a_high, a_low, b_high, b_low, dims):
    return (dot(a_low, b_high, dims) + dot(a_high, b_low, dims)) + dot(a_high, b_high, dims)


NN = ((1,), (0,))
NT = ((1,), (1,))


def fold(value):
    rows = jnp.sum(value, axis=0, keepdims=True)
    return rows[:, 0:128] + rows[:, 128:256] + rows[:, 256:384] + rows[:, 384:512]


def unit_rows(value):
    inverse = lax.rsqrt(jnp.sum(value * value, axis=1, keepdims=True) + epsilon)
    return value * inverse, inverse


def backward(direction, grad, inverse):
    return (grad - direction * jnp.sum(direction * grad, axis=1, keepdims=True)) * inverse


def kernel(
    segments_hbm, futures_hbm, pairs_hbm, log_scale, logit_bias,
    segments_out, futures_out, scalars_out,
    segments, futures, pairs, grad_segments, grad_futures, scalars,
    queries, queries_high, queries_low, keys, keys_high, keys_low,
    weights, weights_high, weights_low, key_terms, x_terms, line_terms,
    query_terms, sibling_terms, y_terms, pair_terms, z_terms, targets,
    sums_group, sums_all,
    in_sem, out_sem, send, kz_recv, kx_recv, qp_recv, qy_recv, qs_recv,
    rx_recv, rz_recv, rs_recv, ry_recv, rp_recv, once_recv,
):
    x, y, z, core = coordinates()
    odd_x, odd_z = lax.rem(x, 2), lax.rem(z, 2)
    sign = 1 - 2 * odd_z
    key_x = x + 1 - 2 * odd_x
    query_x = lax.rem(x + 2 * odd_x + NX - 1, NX)
    pair_z = z + 1 - 2 * odd_z

    sibling = device(x, y, z, 1 - core)
    key_partner = device(key_x, y, z, core)
    query_partner = device(query_x, y, z, core)
    z_partner = device(x, y, pair_z, core)

    def y_device(offset):
        return device(x, lax.rem(y + offset, NY), z, core)

    def line_device(distance, column=None):
        return device(x if column is None else column, y, lax.rem(z + sign * distance + NZ, NZ), core)

    def row_device(offset, other):
        return device(lax.rem(x + offset, NX), y, z, 1 - core if other else core)

    def remote(src, dst, kind, recv, to):
        return pltpu.make_async_remote_copy(
            src_ref=src, dst_ref=dst, send_sem=send.at[kind], recv_sem=recv, device_id=to, device_id_type=MESH
        )

    def await_recv(ref, kind, recv):
        remote(ref, ref, kind, recv, sibling).wait_recv()

    def await_send(ref, kind):
        remote(ref, ref, kind, once_recv.at[0], sibling).wait_send()

    barrier = pltpu.get_barrier_semaphore()
    target_peers = [z_partner, query_partner, device(query_x, y, pair_z, core)]
    row_peers = [(d, other) for d in range(NX) for other in (False, True) if d or other]
    greeted = [line_device(d, column) for d in (2, -2) for column in (None, key_x)]
    greeted += [line_device(-1), z_partner, target_peers[2]]
    greeted += [y_device(d) for d in range(1, NY)] + [row_device(*p) for p in row_peers]
    for other in greeted:
        pl.semaphore_signal(barrier, inc=1, device_id=other, device_id_type=MESH)

    loads = [
        pltpu.make_async_copy(futures_hbm, futures, in_sem.at[0]),
        pltpu.make_async_copy(segments_hbm, segments, in_sem.at[1]),
        pltpu.make_async_copy(pairs_hbm, pairs, in_sem.at[2]),
    ]
    for load in loads:
        load.start()

    def column(combo):
        w = 1 - odd_z if combo in (1, 3) else odd_z
        v = 1 - odd_x if combo in (2, 3) else odd_x
        return w * 2 + v

    def query_slot(combo, offset, c):
        return column(combo) * 8 + lax.rem(y - offset + NY, NY) * 2 + c

    loads[0].wait()
    key_unit, key_inverse = unit_rows(futures[...])
    keys[0] = key_unit
    loads[1].wait()
    query_unit, query_inverse = unit_rows(segments[...])
    queries[query_slot(0, 0, core)] = query_unit
    loads[2].wait()
    mine = pairs[...]
    parts = [
        jnp.where(x // 2 == 0, mine[:, 64 * i : 64 * i + 32], mine[:, 64 * i + 32 : 64 * i + 64]) for i in range(NY)
    ]
    targets[column(0)] = jnp.concatenate(parts, axis=1)
    pl.semaphore_wait(barrier, len(greeted))

    def half_rows(half):
        return pl.ds(half * HALF, HALF)

    def gather_line(place, half):
        rows = half_rows(half)
        return remote(
            keys.at[2 * max(place - 2, 0), rows], keys.at[2 * place, rows],
            KZ, kz_recv.at[place - 1, half], line_device(-1 if place == 1 else 2),
        )

    def gather_far(half):
        rows = half_rows(half)
        return remote(
            keys.at[2 * (FAR - 2), rows], keys.at[2 * FAR + 1, rows], KZ, kx_recv.at[FAR], line_device(2, key_x)
        )

    def gather_x(place):
        return remote(keys.at[2 * place], keys.at[2 * place + 1], KX, kx_recv.at[place], key_partner)

    def step_line(*places):
        for place in places:
            for half in range(HALVES):
                gather_line(place, half).wait_recv()
                if place + 2 <= FAR:
                    gather_line(place + 2, half).start()
                if place + 2 == FAR:
                    gather_far(half).start()
        for place in places:
            if place < FAR:
                gather_x(place).start()

    def await_x(place):
        await_recv(keys.at[2 * place + 1], KX, kx_recv.at[place])

    def gather_partner(combo):
        slot = queries.at[query_slot(0 if combo < 3 else 1, 0, core)]
        return remote(slot, slot, QP, qp_recv.at[combo], z_partner if combo == 1 else query_partner)

    def gather_y(combo, offset):
        slot = queries.at[query_slot(combo, 0, core)]
        return remote(slot, slot, QY, qy_recv.at[combo], y_device(offset))

    def gather_sibling(combo, offset):
        slot = queries.at[query_slot(combo, offset, core)]
        return remote(slot, slot, QS, qs_recv.at[combo], sibling)

    def split_query(slot):
        high, low = split(queries[slot])
        rows = pl.ds(pl.multiple_of(slot * ROWS, ROWS), ROWS)
        queries_high[rows] = high
        queries_low[rows] = low

    def split_keys(first, last):
        high, low = split(keys[first:last].reshape((last - first) * ROWS, WIDTH))
        keys_high[first * ROWS : last * ROWS] = high
        keys_low[first * ROWS : last * ROWS] = low

    def spread(combo):
        if combo > 0:
            gather_partner(combo).wait_recv()
        if combo == 1:
            gather_partner(3).start()
        for offset in (2, 1, 3):
            gather_y(combo, offset).start()
        gather_sibling(combo, 0).start()
        split_query(query_slot(combo, 0, core))

    def take_y(combo):
        await_recv(queries.at[pl.ds(0, 3)], QY, qy_recv.at[combo])
        for offset in (1, 3, 2):
            gather_sibling(combo, offset).start()
        for offset in (1, 3, 2):
            split_query(query_slot(combo, offset, core))

    def take_sibling(combo):
        await_recv(queries.at[pl.ds(0, 4)], QS, qs_recv.at[combo])
        for offset in (0, 1, 3, 2):
            split_query(query_slot(combo, offset, 1 - core))

    for half in range(HALVES):
        gather_line(1, half).start()
        gather_line(2, half).start()
    gather_x(0).start()
    gather_partner(1).start()
    gather_partner(2).start()
    spread(0)
    mine_target = targets.at[column(0)]
    for to in target_peers:
        remote(mine_target, mine_target, TG, once_recv.at[0], to).start()
    scale = jnp.exp(log_scale[...])
    bias = logit_bias[...]
    step_line(1, 2)
    spread(1)
    spread(2)
    take_y(0)
    spread(3)
    step_line(3, 4)
    take_y(1)
    take_sibling(0)
    take_y(2)
    step_line(5, 6)
    take_sibling(1)
    take_y(3)
    take_sibling(2)
    take_sibling(3)
    await_recv(targets.at[pl.ds(0, 3)], TG, once_recv.at[0])

    def pair_block(first, last):
        a, b = first * ROWS, last * ROWS
        raw = dot3(
            keys_high[a:b], keys_low[a:b], queries_high[...], queries_low[...], NT
        )
        value = scale * raw + bias
        row = lax.broadcasted_iota(jnp.int32, (b - a, 1), 0) + a
        place = row // (2 * ROWS)
        line = lax.rem(z + NZ - sign * place, NZ)
        low_x = jnp.where(row // ROWS % 2 == 1, 1 - odd_x, odd_x)
        key_row = (low_x * NZ + line) * (ROWS * 16) + lax.axis_index("ka") * ROWS + row % ROWS
        target = jnp.concatenate([targets[i] for i in range(4)], axis=1)
        hit = key_row == target
        small = jnp.exp(-jnp.abs(value))
        sigmoid = jnp.where(value >= 0, f32(1.0), small) / (f32(1.0) + small)
        weight = sigmoid - hit.astype(f32)
        softplus = jnp.maximum(value, f32(0.0)) + jnp.log1p(small)
        weights[a:b] = scale * weight
        loss = fold(softplus - jnp.where(hit, value, f32(0.0)))
        by_scale = fold(weight * (value - bias))
        by_bias = fold(weight)
        return jnp.concatenate([loss, by_scale, by_bias, jnp.zeros((5, 128), f32)], axis=0)

    def key_block(first, last):
        a, b = first * ROWS, last * ROWS
        high, low = split(weights[a:b])
        out = dot3(high, low, queries_high[...], queries_low[...], NN)
        key_terms[first:last] = out.reshape(last - first, ROWS, WIDTH)

    for place in range(FIRST // 2):
        await_x(place)
    split_keys(0, FIRST)
    totals = pair_block(0, FIRST)
    step_line(7)
    for place in range(FIRST // 2, RING):
        await_x(place)
    split_keys(FIRST, CHIPS)
    totals = totals + pair_block(FIRST, CHIPS)

    def start_group():
        place = column(0) * 8 + y * 2 + core
        sums_group[place] = totals
        slot = sums_group.at[place]
        for i in range(1, 2 * CHIPS):
            far_x, far_z = query_x if i // 8 % 2 else x, pair_z if i // 16 else z
            to = device(far_x, lax.rem(y + i // 2, NY), far_z, lax.rem(core + i, 2))
            remote(slot, slot, SG, once_recv.at[1], to).start()

    start_group()
    key_block(FIRST, CHIPS)

    def sum_x(place):
        return remote(key_terms.at[2 * place + 1], x_terms.at[place], RX, rx_recv.at[place], key_partner)

    def sum_far(half):
        rows = half_rows(half)
        return remote(
            key_terms.at[2 * FAR + 1, rows], x_terms.at[FAR, rows], RX, rx_recv.at[FAR + half], line_device(-2, key_x)
        )

    def sum_line(place, half):
        rows = half_rows(half)
        return remote(
            key_terms.at[2 * place, rows], line_terms.at[place - 1, rows],
            RZ, rz_recv.at[place - 1, half], line_device(-1 if place == 1 else -2),
        )

    def start_x(*places):
        for place in places:
            sum_x(place).start()

    def start_far():
        for half in range(HALVES):
            sum_line(FAR, half).start()
            sum_far(half).start()

    def reduce_line(place):
        sum_x(place).wait_recv()
        for half in range(HALVES):
            rows = half_rows(half)
            total = key_terms[2 * place, rows] + x_terms[place, rows]
            if place + 2 <= FAR:
                sum_line(place + 2, half).wait_recv()
                total = total + line_terms[place + 1, rows]
            if place + 2 == FAR:
                sum_far(half).wait_recv()
                total = total + x_terms[FAR, rows]
            key_terms[2 * place, rows] = total
            sum_line(place, half).start()

    start_far()
    start_x(5, 6)

    def start_all():
        await_recv(sums_group.at[pl.ds(0, 2 * CHIPS - 1)], SG, once_recv.at[1])
        place = z // 2 * 2 + lax.rem((x + 1) // 2, 2)
        sums_all[place] = jnp.sum(sums_group[...], axis=0)
        slot = sums_all.at[place]
        for d in range(RING):
            if d > 0:
                remote(slot, slot, SA, once_recv.at[2], line_device(-d)).start()
            remote(slot, slot, SA, once_recv.at[2], line_device(-d, key_x)).start()

    def finish_scalars():
        await_recv(sums_all.at[pl.ds(0, CHIPS - 1)], SA, once_recv.at[2])
        total = jnp.sum(sums_all[...], axis=0) * f32(1.0 / 8192)
        for i in range(3):
            scalars[i] = jnp.sum(total[i : i + 1, :])

    def query_block(combo):
        rows = pl.ds(pl.multiple_of(column(combo) * 8 * ROWS, 8 * ROWS), 8 * ROWS)
        out = dot3(weights_high[rows], weights_low[rows], keys_high[...], keys_low[...], NN)
        query_terms[combo] = out.reshape(NY, 2, ROWS, WIDTH)
        for place in range(NY):
            remote(
                query_terms.at[combo, place, 1 - core], sibling_terms.at[combo, place],
                RS, rs_recv.at[combo], sibling,
            ).start()

    def sum_y(combo, offset):
        return remote(
            query_terms.at[combo, lax.rem(y + offset, NY), core], y_terms.at[combo, offset],
            RY, ry_recv.at[combo], y_device(offset),
        )

    def start_y(combo):
        await_recv(sibling_terms.at[combo], RS, rs_recv.at[combo])
        for offset in (2, 1, 3, 0):
            place = lax.rem(y + offset, NY)
            query_terms[combo, place, core] = query_terms[combo, place, core] + sibling_terms[combo, place]
            if offset > 0:
                sum_y(combo, offset).start()

    def take_column(combo):
        await_recv(y_terms.at[combo, pl.ds(1, 3)], RY, ry_recv.at[combo])
        return ((y_terms[combo, 1] + y_terms[combo, 3]) + y_terms[combo, 2]) + query_terms[combo, y, core]

    def sum_partner(combo):
        return remote(
            pair_terms.at[combo], z_terms.at[combo], RP, rp_recv.at[combo],
            z_partner if combo == 1 else query_partner,
        )

    high, low = split(weights[...].T)
    weights_high[...] = high
    weights_low[...] = low
    query_block(3)
    query_block(2)
    start_y(3)
    query_block(1)
    start_y(2)
    query_block(0)
    start_y(1)
    reduce_line(6)
    reduce_line(5)
    key_block(0, FIRST)
    start_x(3, 4, 1, 2, 0)
    start_y(0)
    start_all()
    reduce_line(3)
    reduce_line(4)
    for combo in (3, 2):
        pair_terms[combo] = take_column(combo)
        sum_partner(combo).start()
    near = take_column(1)
    sum_partner(3).wait_recv()
    pair_terms[1] = near + z_terms[3]
    sum_partner(1).start()
    reduce_line(1)
    reduce_line(2)

    query_grad = take_column(0)
    sum_partner(2).wait_recv()
    query_grad = query_grad + z_terms[2]
    sum_partner(1).wait_recv()
    query_grad = query_grad + z_terms[1]
    grad_segments[...] = backward(query_unit, query_grad, query_inverse)
    stores = [
        pltpu.make_async_copy(grad_segments, segments_out, out_sem.at[0]),
        pltpu.make_async_copy(scalars, scalars_out, out_sem.at[1]),
        pltpu.make_async_copy(grad_futures, futures_out, out_sem.at[2]),
    ]
    stores[0].start()

    finish_scalars()
    stores[1].start()

    sum_x(0).wait_recv()
    for half in range(HALVES):
        sum_line(1, half).wait_recv()
        sum_line(2, half).wait_recv()
    key_grad = (key_terms[0] + x_terms[0]) + (line_terms[0] + line_terms[1])
    grad_futures[...] = backward(key_unit, key_grad, key_inverse)
    stores[2].start()

    def blocks(ref, count):
        return ref.at[pl.ds(0, count)]

    await_send(blocks(keys, 8), KZ)
    await_send(blocks(keys, 7), KX)
    await_send(blocks(queries, 3), QP)
    await_send(blocks(queries, 12), QY)
    await_send(blocks(queries, 16), QS)
    await_send(blocks(targets, 3), TG)
    await_send(blocks(key_terms, 8), RX)
    await_send(blocks(key_terms, 7), RZ)
    await_send(blocks(queries, 16), RS)
    await_send(blocks(queries, 12), RY)
    await_send(blocks(queries, 3), RP)
    await_send(blocks(sums_group, 2 * CHIPS - 1), SG)
    await_send(blocks(sums_all, CHIPS - 1), SA)
    for store in stores:
        store.wait()


def per_device(segments, futures, pair_index, log_scale, logit_bias):
    dma = pltpu.SemaphoreType.DMA
    vmem = pltpu.VMEM
    block = (ROWS, WIDTH)
    sums = (8, 128)
    in_vmem = pl.BlockSpec(memory_space=pltpu.VMEM)
    in_hbm = pl.BlockSpec(memory_space=pltpu.HBM)

    grad_segments, grad_futures, scalars = pl.pallas_call(
        kernel,
        out_shape=(
            jax.ShapeDtypeStruct(block, f32),
            jax.ShapeDtypeStruct(block, f32),
            jax.ShapeDtypeStruct((3,), f32),
        ),
        in_specs=[in_hbm] * 3 + [in_vmem] * 2,
        out_specs=(in_hbm,) * 3,
        scratch_shapes=[
            vmem(block, f32),
            vmem(block, f32),
            vmem((1, 256), jnp.int32),
            vmem(block, f32),
            vmem(block, f32),
            pltpu.SMEM((3,), f32),
            vmem((CHIPS * 2,) + block, f32),
            vmem((QUERIES, WIDTH), bf16),
            vmem((QUERIES, WIDTH), bf16),
            vmem((CHIPS,) + block, f32),
            vmem((KEYS, WIDTH), bf16),
            vmem((KEYS, WIDTH), bf16),
            vmem((KEYS, QUERIES), f32),
            vmem((QUERIES, KEYS), bf16),
            vmem((QUERIES, KEYS), bf16),
            vmem((CHIPS,) + block, f32),
            vmem((RING,) + block, f32),
            vmem((FAR,) + block, f32),
            vmem((4, NY, 2) + block, f32),
            vmem((4, NY) + block, f32),
            vmem((4, NY) + block, f32),
            vmem((4,) + block, f32),
            vmem((4,) + block, f32),
            vmem((4, 1, 128), jnp.int32),
            vmem((2 * CHIPS,) + sums, f32),
            vmem((CHIPS,) + sums, f32),
            dma((3,)),
            dma((3,)),
            dma((13,)),
            dma((FAR, HALVES)),
            dma((RING,)),
            dma((4,)),
            dma((4,)),
            dma((4,)),
            dma((RING + 1,)),
            dma((FAR, HALVES)),
            dma((4,)),
            dma((4,)),
            dma((4,)),
            dma((3,)),
        ],
        compiler_params=pltpu.CompilerParams(
            collective_id=0, has_side_effects=True, vmem_limit_bytes=55060 << 10
        ),
    )(
        segments,
        futures,
        pair_index.reshape(1, 256),
        log_scale.reshape(1, 1),
        logit_bias.reshape(1, 1),
    )
    return grad_segments, grad_futures, scalars


def solution(mesh):
    in_specs = (P(("pb", "ka"), None), P(("pb", "ka"), None), P("pb"), P(), P())
    out_specs = (P(("pb", "ka"), None), P(("pb", "ka"), None), P())
    return jax.shard_map(
        per_device, mesh=mesh, in_specs=in_specs, out_specs=out_specs, check_vma=False
    )
```
